32 devices in a mesh: hours: 2 (over x), chan: 2 (over core), freq: 8 (over z, y).
Axes of the slice: x: 2, y: 2, z: 4, core: 2. Of those that a mesh axis runs over, the one named last changes fastest.
Arguments:
- samples: bfloat16 [1152, 32, 1024], P('chan', ('hours', 'freq')), parts along dimension 1, may hold values from -18 to 18
Outputs:
- cross_spectra: bfloat16 [2, 256, 1152, 1152], P(None, ('hours', 'freq'), None, 'chan'), parts along dimension 1
The draws below stay inside these ranges and needn't reach their ends.
There are 2 independent parts, one for each index of `hours`. The reference program is written for one: setup_inputs(seed, part) draws one part's arguments, and reference() takes and returns one part's arrays. A program takes and returns all parts, laid end to end along the dimension named above; each array names one. Nothing has to cross between parts.
All inputs are finite; a program needn't handle non-finite values.
Results may differ from the reference program's by a relative error of at most 0.008.
Values may be sent and summed in bfloat16 or wider, within the bound.
A program may use at most 192 MiB of HBM per device.

```python
import math
import jax
import jax.numpy as jnp
from jax import lax

CHANNELS = 1152
SAMPLES = 1024
BINS = 128
WINDOWS = 16


def draw_samples(key, part):
    first, second = jax.random.split(jax.random.fold_in(key, 7), 2)
    gains = jnp.exp(jax.random.uniform(first, (CHANNELS, 1, 1), jnp.float32, math.log(0.1), math.log(3.0)))
    values = jnp.clip(jax.random.normal(second, (CHANNELS, WINDOWS, SAMPLES), jnp.float32), -6.0, 6.0)
    return (gains * values).astype(jnp.bfloat16)


def setup_inputs(seed: int = 0, part: int = 0) -> dict:
    arg_keys = jax.random.split(jax.random.key(seed), 2)
    part_keys = jax.random.split(jax.random.fold_in(arg_keys[1], part), 2)
    samples = draw_samples(jax.random.fold_in(jax.random.fold_in(arg_keys[1], part), 71), part)
    return dict(samples=samples)


def bin_table(length, bins):
    position = lax.broadcasted_iota(jnp.int32, (length, bins), 0)
    number = lax.broadcasted_iota(jnp.int32, (length, bins), 1) + 1
    phase = (position * number % length).astype(jnp.float32) * (2.0 * math.pi / length)
    taper = 0.5 - 0.5 * jnp.cos(position.astype(jnp.float32) * (2.0 * math.pi / length))
    factor = math.sqrt(8.0 / (3.0 * length))
    table = jnp.concatenate([taper * jnp.cos(phase), -(taper * jnp.sin(phase))], axis=1) * factor
    return table.astype(jnp.bfloat16)

def whiten(padded, first_bin, total_bins):
    count_bins = padded.shape[1] - 4
    values = padded.astype(jnp.float32)
    power = values[0] * values[0] + values[1] * values[1]
    summed = power[0:count_bins] + power[1:count_bins + 1]
    summed = summed + power[2:count_bins + 2]
    summed = summed + power[3:count_bins + 3]
    summed = summed + power[4:count_bins + 4]
    which = first_bin + jnp.arange(count_bins, dtype=jnp.int32)
    upper = jnp.minimum(which + 2, total_bins - 1)
    lower = jnp.maximum(which - 2, 0)
    count = (upper - lower + 1).astype(jnp.float32)
    level = jnp.maximum(summed / count[:, None, None], 0.1)
    return (values[:, 2:count_bins + 2] / jnp.sqrt(level)[None]).astype(jnp.bfloat16)

def reference(samples):
    channels, windows, length = samples.shape
    table = bin_table(length, BINS)
    flat = jnp.dot(samples.reshape(channels * windows, length), table, preferred_element_type=jnp.float32)
    spectrum = flat.reshape(channels, windows, 2, BINS).transpose(2, 3, 1, 0).astype(jnp.bfloat16)
    padded = jnp.pad(spectrum, ((0, 0), (2, 2), (0, 0), (0, 0)))
    whitened = whiten(padded, 0, BINS)

    def one_bin(index):
        single = lax.dynamic_index_in_dim(whitened, index, 1, keepdims=False).astype(jnp.float32)
        real_part = jnp.einsum('pwa,pwb->ab', single, single)
        rotated = jnp.stack([-single[1], single[0]])
        imag_part = jnp.einsum('pwa,pwb->ab', single, rotated)
        return (jnp.stack([real_part, imag_part]) / windows).astype(jnp.bfloat16)
    stacked = lax.map(one_bin, jnp.arange(BINS, dtype=jnp.int32))
    return jnp.transpose(stacked, (1, 0, 3, 2))
```

```python
import functools
import math

import jax
import jax.numpy as jnp
import numpy as np
from jax import lax
from jax.experimental import pallas as pl
from jax.experimental.pallas import tpu as pltpu
from jax.sharding import PartitionSpec as P

BINS = 128
LANES = 128
MESH = pl.DeviceIdType.MESH


def bin_table(length, bins):
    position = np.arange(length, dtype=np.int64)[:, None]
    number = np.arange(bins, dtype=np.int64)[None, :] + 1
    step = np.float32(2.0 * math.pi / length)
    phase = (position * number % length).astype(np.float32) * step
    half = np.float32(0.5)
    taper = half - half * np.cos(position.astype(np.float32) * step)
    factor = np.float32(math.sqrt(8.0 / (3.0 * length)))
    table = np.concatenate([taper * np.cos(phase), -(taper * np.sin(phase))], axis=1) * factor
    return jnp.asarray(table.astype(np.float32)).astype(jnp.bfloat16)


def whiten(real, imag):
    bins = real.shape[0]
    power = real * real + imag * imag
    row = lax.broadcasted_iota(jnp.int32, (bins, 1), 0)
    summed = power
    for shift in (1, 2):
        summed = summed + jnp.where(row >= shift, pltpu.roll(power, shift, 0), 0.0)
        summed = summed + jnp.where(row < bins - shift, pltpu.roll(power, bins - shift, 0), 0.0)
    count = jnp.minimum(row + 2, bins - 1) - jnp.maximum(row - 2, 0) + 1
    level = jnp.maximum(summed * (1.0 / count.astype(jnp.float32)), 0.1)
    scale = lax.rsqrt(level)
    return real * scale, imag * scale


def chunks_of(channels):
    cut = channels // (2 * LANES) * LANES
    return ((0, cut), (cut, channels)) if cut else ((0, channels),)


def pack(real, imag):
    cut = real.shape[1] // LANES * LANES
    if cut == real.shape[1]:
        return jnp.concatenate([real, imag], axis=1)
    return jnp.concatenate([real[:, :cut], imag[:, :cut], real[:, cut:], imag[:, cut:]], axis=1)


def unpack(values, part):
    channels = values.shape[1] // 2
    cut = channels // LANES * LANES
    rest = channels - cut
    tail = 2 * cut + part * rest
    main = values[:, part * cut : (part + 1) * cut]
    return jnp.concatenate([main, values[:, tail : tail + rest]], axis=1) if rest else main


def spread(tiles, first_row, values):
    height, width = values.shape
    for t in range(pl.cdiv(width, LANES)):
        part = values[:, t * LANES : min((t + 1) * LANES, width)]
        if part.shape[1] < LANES:
            gap = jnp.zeros((height, LANES - part.shape[1]), part.dtype)
            part = jnp.concatenate([part, gap], axis=1)
        tiles[t, pl.ds(first_row, height), :] = part


def exchange_kernel(count, samples_ref, table_ref, mine_ref, every_ref, samples, table, flat, *rest):
    chunks = chunks_of(samples_ref.shape[0])
    n = len(chunks)
    white, own, other = rest[:n], rest[n : 2 * n], rest[2 * n : 3 * n]
    load_sem, send_sem, recv_sem, pass_sem, got_sem = rest[3 * n :]
    hour = lax.axis_index("hours")
    chan = lax.axis_index("chan")
    me = lax.axis_index("freq")
    windows = samples_ref.shape[1]
    local_bins = BINS // count
    rows = windows * local_bins
    total = rows * count
    scale = 1.0 / (windows * count)
    steps = sorted(range(1, count), key=lambda step: abs(2 * step - count))

    loads = [pltpu.make_async_copy(table_ref, table, load_sem.at[n])]
    for c, (low, high) in enumerate(chunks):
        here = pl.ds(low, high - low)
        loads.append(pltpu.make_async_copy(samples_ref.at[here], samples.at[here], load_sem.at[c]))
    for load in loads:
        load.start()

    barrier = pltpu.get_barrier_semaphore()
    for step in steps:
        peer = lax.rem(me + step, count)
        pl.semaphore_signal(barrier, inc=1, device_id=(hour, chan, peer), device_id_type=MESH)
    pl.semaphore_signal(barrier, inc=1, device_id=(hour, 1 - chan, me), device_id_type=MESH)

    sends, passes = {}, {}

    def forward(c, step, source_ref, owner):
        copy = pltpu.make_async_remote_copy(
            src_ref=source_ref,
            dst_ref=other[c].at[owner],
            send_sem=pass_sem.at[c, step],
            recv_sem=got_sem.at[c, step],
            device_id=(hour, 1 - chan, me),
            device_id_type=MESH,
        )
        copy.start()
        passes[c, step] = copy

    loads[0].wait()
    for c, (low, high) in enumerate(chunks):
        size = high - low
        loads[1 + c].wait()
        values = samples[low:high].reshape(size * windows, samples.shape[2])
        product = jnp.dot(values, table[...], preferred_element_type=jnp.float32)
        for part in range(2):
            flat[part, : size * windows] = product[:, part * BINS : (part + 1) * BINS]
        for w in range(windows):
            pick = pl.ds(w, size, stride=windows)
            real = flat[0, pick, :].astype(jnp.bfloat16).T.astype(jnp.float32)
            imag = flat[1, pick, :].astype(jnp.bfloat16).T.astype(jnp.float32)
            packed = pack(*whiten(real, imag)).astype(jnp.bfloat16)
            white[c][:, w] = packed.reshape(count, local_bins, 2 * size)
        if c == 0:
            pl.semaphore_wait(barrier, count)
        for step in steps:
            peer = lax.rem(me + step, count)
            copy = pltpu.make_async_remote_copy(
                src_ref=white[c].at[peer],
                dst_ref=own[c].at[me],
                send_sem=send_sem.at[c, step],
                recv_sem=recv_sem.at[c, step],
                device_id=(hour, chan, peer),
                device_id_type=MESH,
            )
            copy.start()
            sends[c, step] = copy
        forward(c, 0, white[c].at[me], me)

    def settle(step):
        owner = lax.rem(me - step + count, count)
        mine, theirs = [], []
        for c in range(n):
            width = white[c].shape[3]
            source = own[c] if step else white[c]
            passes[c, step].wait_recv()
            mine.append(source[owner].astype(jnp.float32).reshape(rows, width))
            theirs.append(other[c][owner].astype(jnp.float32).reshape(rows, width))
        for part in range(2):
            here = jnp.concatenate([unpack(x, part) for x in mine], axis=1)
            there = jnp.concatenate([unpack(x, part) for x in theirs], axis=1)
            first_row = pl.multiple_of(part * total + owner * rows, 8)
            spread(mine_ref, first_row, here * scale)
            pair = [jnp.where(chan == 0, here, there), jnp.where(chan == 0, there, here)]
            spread(every_ref, first_row, jnp.concatenate(pair, axis=1))

    waiting = [0]
    for step in reversed(steps):
        owner = lax.rem(me - step + count, count)
        for c in range(n):
            sends[c, step].wait_recv()
            forward(c, step, own[c].at[owner], owner)
        waiting.append(step)
        if len(waiting) > 2:
            settle(waiting.pop(0))
    for step in waiting:
        settle(step)
    for copy in sends.values():
        copy.wait_send()
    for copy in passes.values():
        copy.wait_send()


def exchange(samples, table, count):
    channels, windows, length = samples.shape
    local_bins = BINS // count
    rows = 2 * windows * count * local_bins
    chunks = chunks_of(channels)
    n = len(chunks)
    blocks = [
        pltpu.VMEM((count, windows, local_bins, 2 * (high - low)), jnp.bfloat16)
        for low, high in chunks
    ]
    largest = max(high - low for low, high in chunks)
    pieces = pltpu.SemaphoreType.DMA((n, count))
    whole = pl.BlockSpec(memory_space=pltpu.VMEM)
    return pl.pallas_call(
        functools.partial(exchange_kernel, count),
        out_shape=(
            jax.ShapeDtypeStruct((pl.cdiv(channels, LANES), rows, LANES), jnp.float32),
            jax.ShapeDtypeStruct((pl.cdiv(2 * channels, LANES), rows, LANES), jnp.float32),
        ),
        in_specs=[pl.BlockSpec(memory_space=pltpu.HBM), pl.BlockSpec(memory_space=pltpu.HBM)],
        out_specs=(whole, whole),
        scratch_shapes=[
            pltpu.VMEM(samples.shape, samples.dtype),
            pltpu.VMEM(table.shape, table.dtype),
            pltpu.VMEM((2, largest * windows, BINS), jnp.float32),
            *blocks,
            *blocks,
            *blocks,
            pltpu.SemaphoreType.DMA((n + 1,)),
            pieces,
            pieces,
            pieces,
            pieces,
        ],
        compiler_params=pltpu.CompilerParams(
            collective_id=0, has_side_effects=True, vmem_limit_bytes=40 << 20
        ),
        cost_estimate=pl.CostEstimate(
            flops=2 * samples.size * 2 * BINS, bytes_accessed=2 * samples.size, transcendentals=0
        ),
        name="exchange",
    )(samples, table)


def cross_kernel(mine_ref, every_ref, out_ref, held, sems):
    slots, step_bins, _, channels, width = held.shape
    step = pl.program_id(0)
    steps = out_ref.shape[1] // step_bins
    local_bins = steps * step_bins
    windows = mine_ref.shape[1] // (2 * local_bins)
    slot = lax.rem(step, slots)

    def copies(b, part, at_step, at_slot):
        return pltpu.make_async_copy(
            held.at[at_slot, b, part],
            out_ref.at[part, at_step * step_bins + b],
            sems.at[at_slot, b, part],
        )

    pieces = [(b, part) for b in range(step_bins) for part in range(2)]

    @pl.when(step >= slots)
    def _():
        for b, part in pieces:
            copies(b, part, step - slots, slot).wait()

    for b in range(step_bins):
        pick = pl.ds(step * step_bins + b, 2 * windows, stride=local_bins)
        here = [mine_ref[t, pick, :] for t in range(mine_ref.shape[0])]
        here = jnp.concatenate(here, axis=1)[:, :channels]
        left = here.astype(jnp.bfloat16)
        swapped = jnp.concatenate([here[windows:], -here[:windows]], axis=0).astype(jnp.bfloat16)
        right = [every_ref[t, pick, :].astype(jnp.bfloat16) for t in range(every_ref.shape[0])]
        right = jnp.concatenate(right, axis=1)[:, :width]
        for part, side in ((0, left), (1, swapped)):
            product = lax.dot_general(
                side, right, (((0,), (0,)), ((), ())), preferred_element_type=jnp.float32
            )
            held[slot, b, part] = product.astype(jnp.bfloat16)
            copies(b, part, step, slot).start()

    @pl.when(step == steps - 1)
    def _():
        for back in reversed(range(slots)):
            last = steps - 1 - back
            for b, part in pieces:
                copies(b, part, last, last % slots).wait()


def cross(mine, every, windows, channels):
    rows = mine.shape[1]
    local_bins = rows // (2 * windows)
    width = 2 * channels
    step_bins = 2 if local_bins % 2 == 0 else 1
    steps = local_bins // step_bins
    slots = min(2, steps)
    shape = (2, local_bins, channels, width)
    whole = pl.BlockSpec(memory_space=pltpu.VMEM)
    return pl.pallas_call(
        cross_kernel,
        grid=(steps,),
        out_shape=jax.ShapeDtypeStruct(shape, jnp.bfloat16),
        in_specs=[whole, whole],
        out_specs=pl.BlockSpec(memory_space=pl.ANY),
        scratch_shapes=[
            pltpu.VMEM((slots, step_bins, 2, channels, width), jnp.bfloat16),
            pltpu.SemaphoreType.DMA((slots, step_bins, 2)),
        ],
        compiler_params=pltpu.CompilerParams(vmem_limit_bytes=50 << 20),
        cost_estimate=pl.CostEstimate(
            flops=2 * rows * channels * width * 2,
            bytes_accessed=2 * math.prod(shape),
            transcendentals=0,
        ),
        name="cross",
    )(mine, every)


def local(samples):
    channels, windows, length = samples.shape
    count = lax.axis_size("freq")
    samples = pltpu.with_memory_space_constraint(samples, pltpu.HBM)
    table = pltpu.with_memory_space_constraint(bin_table(length, BINS), pltpu.HBM)
    mine, every = exchange(samples, table, count)
    return jnp.swapaxes(cross(mine, every, windows * count, channels), 2, 3)


def solution(mesh):
    return jax.shard_map(
        local,
        mesh=mesh,
        in_specs=(P("chan", ("hours", "freq"), None),),
        out_specs=P(None, ("hours", "freq"), None, "chan"),
        check_vma=False,
    )
```

```python
import functools
import math

import jax
import jax.numpy as jnp
import numpy as np
from jax import lax
from jax.experimental import pallas as pl
from jax.experimental.pallas import tpu as pltpu
from jax.sharding import PartitionSpec as P

BINS = 128
LANES = 128
MESH = pl.DeviceIdType.MESH


def bin_table(length, bins):
    position = np.arange(length, dtype=np.int64)[:, None]
    number = np.arange(bins, dtype=np.int64)[None, :] + 1
    step = np.float32(2.0 * math.pi / length)
    phase = (position * number % length).astype(np.float32) * step
    half = np.float32(0.5)
    taper = half - half * np.cos(position.astype(np.float32) * step)
    factor = np.float32(math.sqrt(8.0 / (3.0 * length)))
    table = np.concatenate([taper * np.cos(phase), -(taper * np.sin(phase))], axis=1) * factor
    return jnp.asarray(table.astype(np.float32)).astype(jnp.bfloat16)


def whiten(real, imag):
    bins = real.shape[0]
    power = real * real + imag * imag
    row = lax.broadcasted_iota(jnp.int32, (bins, 1), 0)
    summed = power
    for shift in (1, 2):
        summed = summed + jnp.where(row >= shift, pltpu.roll(power, shift, 0), 0.0)
        summed = summed + jnp.where(row < bins - shift, pltpu.roll(power, bins - shift, 0), 0.0)
    count = jnp.minimum(row + 2, bins - 1) - jnp.maximum(row - 2, 0) + 1
    level = jnp.maximum(summed * (1.0 / count.astype(jnp.float32)), 0.1)
    scale = lax.rsqrt(level)
    return real * scale, imag * scale


def chunks_of(channels):
    return ((0, LANES), (LANES, channels)) if channels > LANES else ((0, channels),)


def order_of(count):
    return sorted(range(1, count), key=lambda mask: (-mask.bit_length(), mask))


def partner(me, mask, count):
    bits = count.bit_length() - 1
    other = 0
    for bit in range(bits):
        digit = lax.rem(me // (1 << bit), 2)
        other = other + (1 << bit) * ((1 - digit) if mask >> bit & 1 else digit)
    return other


def pack(real, imag):
    cut = real.shape[1] // LANES * LANES
    if cut == real.shape[1]:
        return jnp.concatenate([real, imag], axis=1)
    return jnp.concatenate([real[:, :cut], imag[:, :cut], real[:, cut:], imag[:, cut:]], axis=1)


def unpack(values, part):
    channels = values.shape[1] // 2
    cut = channels // LANES * LANES
    rest = channels - cut
    tail = 2 * cut + part * rest
    main = values[:, part * cut : (part + 1) * cut]
    return jnp.concatenate([main, values[:, tail : tail + rest]], axis=1) if rest else main


def spread(tiles, first_row, values):
    height, width = values.shape
    for t in range(pl.cdiv(width, LANES)):
        part = values[:, t * LANES : min((t + 1) * LANES, width)]
        if part.shape[1] < LANES:
            gap = jnp.zeros((height, LANES - part.shape[1]), part.dtype)
            part = jnp.concatenate([part, gap], axis=1)
        tiles[t, pl.ds(first_row, height), :] = part


def exchange_kernel(count, samples_ref, table_ref, mine_ref, every_ref, samples, table, flat, *rest):
    chunks = chunks_of(samples_ref.shape[0])
    n = len(chunks)
    white, own, other = rest[:n], rest[n : 2 * n], rest[2 * n : 3 * n]
    load_sem, send_sem, recv_sem, pass_sem, got_sem = rest[3 * n :]
    hour = lax.axis_index("hours")
    chan = lax.axis_index("chan")
    me = lax.axis_index("freq")
    windows = samples_ref.shape[1]
    local_bins = BINS // count
    rows = windows * local_bins
    total = rows * count
    scale = 1.0 / (windows * count)
    steps = order_of(count)
    peers = {step: partner(me, step, count) for step in range(count)}

    loads = [pltpu.make_async_copy(table_ref, table, load_sem.at[n])]
    for c, (low, high) in enumerate(chunks):
        here = pl.ds(low, high - low)
        loads.append(pltpu.make_async_copy(samples_ref.at[here], samples.at[here], load_sem.at[c]))
    for load in loads[:2]:
        load.start()

    barrier = pltpu.get_barrier_semaphore()
    for step in steps:
        peer = peers[step]
        pl.semaphore_signal(barrier, inc=1, device_id=(hour, chan, peer), device_id_type=MESH)
    pl.semaphore_signal(barrier, inc=1, device_id=(hour, 1 - chan, me), device_id_type=MESH)

    sends, passes = {}, {}

    def forward(c, step, source_ref, owner):
        copy = pltpu.make_async_remote_copy(
            src_ref=source_ref,
            dst_ref=other[c].at[owner],
            send_sem=pass_sem.at[c, step],
            recv_sem=got_sem.at[c, step],
            device_id=(hour, 1 - chan, me),
            device_id_type=MESH,
        )
        copy.start()
        passes[c, step] = copy

    far = [step for step in steps if 2 * step >= count]
    near = [step for step in steps if 2 * step < count]

    def send(c, steps):
        for step in steps:
            peer = peers[step]
            copy = pltpu.make_async_remote_copy(
                src_ref=white[c].at[peer],
                dst_ref=own[c].at[me],
                send_sem=send_sem.at[c, step],
                recv_sem=recv_sem.at[c, step],
                device_id=(hour, chan, peer),
                device_id_type=MESH,
            )
            copy.start()
            sends[c, step] = copy

    loads[0].wait()
    for load in loads[2:]:
        load.start()
    for c, (low, high) in enumerate(chunks):
        size = high - low
        loads[1 + c].wait()
        values = samples[low:high].reshape(size * windows, samples.shape[2])
        product = jnp.dot(values, table[...], preferred_element_type=jnp.float32)
        for part in range(2):
            flat[part, : size * windows] = product[:, part * BINS : (part + 1) * BINS]
        for w in range(windows):
            pick = pl.ds(w, size, stride=windows)
            real = flat[0, pick, :].astype(jnp.bfloat16).T.astype(jnp.float32)
            imag = flat[1, pick, :].astype(jnp.bfloat16).T.astype(jnp.float32)
            packed = pack(*whiten(real, imag)).astype(jnp.bfloat16)
            white[c][:, w] = packed.reshape(count, local_bins, 2 * size)
        if c == 0:
            pl.semaphore_wait(barrier, count)
        send(c, far)
        forward(c, 0, white[c].at[me], me)

    for c in range(n):
        send(c, near)

    def settle(step):
        owner = peers[step]
        mine, theirs = [], []
        for c in range(n):
            width = white[c].shape[3]
            source = own[c] if step else white[c]
            passes[c, step].wait_recv()
            mine.append(source[owner].astype(jnp.float32).reshape(rows, width))
            theirs.append(other[c][owner].astype(jnp.float32).reshape(rows, width))
        for part in range(2):
            here = jnp.concatenate([unpack(x, part) for x in mine], axis=1)
            there = jnp.concatenate([unpack(x, part) for x in theirs], axis=1)
            first_row = pl.multiple_of(part * total + owner * rows, 8)
            spread(mine_ref, first_row, here * scale)
            pair = [jnp.where(chan == 0, here, there), jnp.where(chan == 0, there, here)]
            spread(every_ref, first_row, jnp.concatenate(pair, axis=1))

    waiting = [0]
    for step in range(1, count):
        owner = peers[step]
        for c in range(n):
            sends[c, step].wait_recv()
            forward(c, step, own[c].at[owner], owner)
        waiting.append(step)
        if len(waiting) > 2:
            settle(waiting.pop(0))
    for step in waiting:
        settle(step)
    for copy in sends.values():
        copy.wait_send()
    for copy in passes.values():
        copy.wait_send()


def exchange(samples, table, count):
    channels, windows, length = samples.shape
    local_bins = BINS // count
    rows = 2 * windows * count * local_bins
    chunks = chunks_of(channels)
    n = len(chunks)
    blocks = [
        pltpu.VMEM((count, windows, local_bins, 2 * (high - low)), jnp.bfloat16)
        for low, high in chunks
    ]
    largest = max(high - low for low, high in chunks)
    pieces = pltpu.SemaphoreType.DMA((n, count))
    whole = pl.BlockSpec(memory_space=pltpu.VMEM)
    return pl.pallas_call(
        functools.partial(exchange_kernel, count),
        out_shape=(
            jax.ShapeDtypeStruct((pl.cdiv(channels, LANES), rows, LANES), jnp.float32),
            jax.ShapeDtypeStruct((pl.cdiv(2 * channels, LANES), rows, LANES), jnp.float32),
        ),
        in_specs=[pl.BlockSpec(memory_space=pltpu.HBM), pl.BlockSpec(memory_space=pltpu.HBM)],
        out_specs=(whole, whole),
        scratch_shapes=[
            pltpu.VMEM(samples.shape, samples.dtype),
            pltpu.VMEM(table.shape, table.dtype),
            pltpu.VMEM((2, largest * windows, BINS), jnp.float32),
            *blocks,
            *blocks,
            *blocks,
            pltpu.SemaphoreType.DMA((n + 1,)),
            pieces,
            pieces,
            pieces,
            pieces,
        ],
        compiler_params=pltpu.CompilerParams(
            collective_id=0, has_side_effects=True, vmem_limit_bytes=40 << 20
        ),
        cost_estimate=pl.CostEstimate(
            flops=2 * samples.size * 2 * BINS, bytes_accessed=2 * samples.size, transcendentals=0
        ),
        name="exchange",
    )(samples, table)


def cross_kernel(mine_ref, every_ref, out_ref, held, sems):
    slots, step_bins, _, channels, width = held.shape
    step = pl.program_id(0)
    steps = out_ref.shape[1] // step_bins
    local_bins = steps * step_bins
    windows = mine_ref.shape[1] // (2 * local_bins)
    slot = lax.rem(step, slots)

    def copies(b, part, at_step, at_slot):
        return pltpu.make_async_copy(
            held.at[at_slot, b, part],
            out_ref.at[part, at_step * step_bins + b],
            sems.at[at_slot, b, part],
        )

    pieces = [(b, part) for b in range(step_bins) for part in range(2)]

    @pl.when(step >= slots)
    def _():
        for b, part in pieces:
            copies(b, part, step - slots, slot).wait()

    for b in range(step_bins):
        pick = pl.ds(step * step_bins + b, 2 * windows, stride=local_bins)
        here = [mine_ref[t, pick, :] for t in range(mine_ref.shape[0])]
        here = jnp.concatenate(here, axis=1)[:, :channels]
        left = here.astype(jnp.bfloat16)
        swapped = jnp.concatenate([here[windows:], -here[:windows]], axis=0).astype(jnp.bfloat16)
        right = [every_ref[t, pick, :].astype(jnp.bfloat16) for t in range(every_ref.shape[0])]
        right = jnp.concatenate(right, axis=1)[:, :width]
        for part, side in ((0, left), (1, swapped)):
            product = lax.dot_general(
                side, right, (((0,), (0,)), ((), ())), preferred_element_type=jnp.float32
            )
            held[slot, b, part] = product.astype(jnp.bfloat16)
            copies(b, part, step, slot).start()

    @pl.when(step == steps - 1)
    def _():
        for back in reversed(range(slots)):
            last = steps - 1 - back
            for b, part in pieces:
                copies(b, part, last, last % slots).wait()


def cross(mine, every, windows, channels):
    rows = mine.shape[1]
    local_bins = rows // (2 * windows)
    width = 2 * channels
    step_bins = 2 if local_bins % 2 == 0 else 1
    steps = local_bins // step_bins
    slots = min(2, steps)
    shape = (2, local_bins, channels, width)
    whole = pl.BlockSpec(memory_space=pltpu.VMEM)
    return pl.pallas_call(
        cross_kernel,
        grid=(steps,),
        out_shape=jax.ShapeDtypeStruct(shape, jnp.bfloat16),
        in_specs=[whole, whole],
        out_specs=pl.BlockSpec(memory_space=pl.ANY),
        scratch_shapes=[
            pltpu.VMEM((slots, step_bins, 2, channels, width), jnp.bfloat16),
            pltpu.SemaphoreType.DMA((slots, step_bins, 2)),
        ],
        compiler_params=pltpu.CompilerParams(vmem_limit_bytes=50 << 20),
        cost_estimate=pl.CostEstimate(
            flops=2 * rows * channels * width * 2,
            bytes_accessed=2 * math.prod(shape),
            transcendentals=0,
        ),
        name="cross",
    )(mine, every)


def local(samples):
    channels, windows, length = samples.shape
    count = lax.axis_size("freq")
    samples = pltpu.with_memory_space_constraint(samples, pltpu.HBM)
    table = pltpu.with_memory_space_constraint(bin_table(length, BINS), pltpu.HBM)
    mine, every = exchange(samples, table, count)
    return jnp.swapaxes(cross(mine, every, windows * count, channels), 2, 3)


def solution(mesh):
    return jax.shard_map(
        local,
        mesh=mesh,
        in_specs=(P("chan", ("hours", "freq"), None),),
        out_specs=P(None, ("hours", "freq"), None, "chan"),
        check_vma=False,
    )
```

```python
import functools
import math

import jax
import jax.numpy as jnp
import numpy as np
from jax import lax
from jax.experimental import pallas as pl
from jax.experimental.pallas import tpu as pltpu
from jax.sharding import PartitionSpec as P

BINS = 128
LANES = 128
MESH = pl.DeviceIdType.MESH


def bin_table(length, bins):
    position = np.arange(length, dtype=np.int64)[:, None]
    number = np.arange(bins, dtype=np.int64)[None, :] + 1
    step = np.float32(2.0 * math.pi / length)
    phase = (position * number % length).astype(np.float32) * step
    half = np.float32(0.5)
    taper = half - half * np.cos(position.astype(np.float32) * step)
    factor = np.float32(math.sqrt(8.0 / (3.0 * length)))
    table = np.concatenate([taper * np.cos(phase), -(taper * np.sin(phase))], axis=1) * factor
    return jnp.asarray(table.astype(np.float32)).astype(jnp.bfloat16)


def whiten(real, imag):
    bins = real.shape[0]
    power = real * real + imag * imag
    row = lax.broadcasted_iota(jnp.int32, (bins, 1), 0)
    summed = power
    for shift in (1, 2):
        summed = summed + jnp.where(row >= shift, pltpu.roll(power, shift, 0), 0.0)
        summed = summed + jnp.where(row < bins - shift, pltpu.roll(power, bins - shift, 0), 0.0)
    count = jnp.minimum(row + 2, bins - 1) - jnp.maximum(row - 2, 0) + 1
    level = jnp.maximum(summed * (1.0 / count.astype(jnp.float32)), 0.1)
    scale = lax.rsqrt(level)
    return real * scale, imag * scale


def chunks_of(channels):
    return ((0, LANES), (LANES, channels)) if channels > LANES else ((0, channels),)


def order_of(count):
    return sorted(range(1, count), key=lambda mask: (-mask.bit_length(), mask ^ (mask >> 1 & 1)))


def partner(me, mask, count):
    bits = count.bit_length() - 1
    other = 0
    for bit in range(bits):
        digit = lax.rem(me // (1 << bit), 2)
        other = other + (1 << bit) * ((1 - digit) if mask >> bit & 1 else digit)
    return other


def pack(real, imag):
    cut = real.shape[1] // LANES * LANES
    if cut == real.shape[1]:
        return jnp.concatenate([real, imag], axis=1)
    return jnp.concatenate([real[:, :cut], imag[:, :cut], real[:, cut:], imag[:, cut:]], axis=1)


def unpack(values, part):
    channels = values.shape[1] // 2
    cut = channels // LANES * LANES
    rest = channels - cut
    tail = 2 * cut + part * rest
    main = values[:, part * cut : (part + 1) * cut]
    return jnp.concatenate([main, values[:, tail : tail + rest]], axis=1) if rest else main


def spread(tiles, first_row, values):
    height, width = values.shape
    for t in range(pl.cdiv(width, LANES)):
        part = values[:, t * LANES : min((t + 1) * LANES, width)]
        if part.shape[1] < LANES:
            gap = jnp.zeros((height, LANES - part.shape[1]), part.dtype)
            part = jnp.concatenate([part, gap], axis=1)
        tiles[t, pl.ds(first_row, height), :] = part


def exchange_kernel(count, samples_ref, table_ref, mine_ref, every_ref, samples, table, flat,
                    white, own, other, load_sem, send_sem, recv_sem, pass_sem, got_sem):
    chunks = chunks_of(samples_ref.shape[0])
    n = len(chunks)
    hour = lax.axis_index("hours")
    chan = lax.axis_index("chan")
    me = lax.axis_index("freq")
    windows = samples_ref.shape[1]
    local_bins = BINS // count
    rows = windows * local_bins
    total = rows * count
    scale = 1.0 / (windows * count)
    steps = order_of(count)
    peers = {step: partner(me, step, count) for step in range(count)}

    loads = [pltpu.make_async_copy(table_ref, table, load_sem.at[n])]
    for c, (low, high) in enumerate(chunks):
        here = pl.ds(low, high - low)
        loads.append(pltpu.make_async_copy(samples_ref.at[here], samples.at[here], load_sem.at[c]))
    for load in loads[:2]:
        load.start()

    barrier = pltpu.get_barrier_semaphore()
    for step in steps:
        peer = peers[step]
        pl.semaphore_signal(barrier, inc=1, device_id=(hour, chan, peer), device_id_type=MESH)
    pl.semaphore_signal(barrier, inc=1, device_id=(hour, 1 - chan, me), device_id_type=MESH)

    sends, passes = {}, {}

    def forward(step, source_ref, owner):
        copy = pltpu.make_async_remote_copy(
            src_ref=source_ref,
            dst_ref=other.at[owner],
            send_sem=pass_sem.at[step],
            recv_sem=got_sem.at[step],
            device_id=(hour, 1 - chan, me),
            device_id_type=MESH,
        )
        copy.start()
        passes[step] = copy

    far = [step for step in steps if 2 * step >= count]
    near = [step for step in steps if 2 * step < count]

    def send(c, steps, low, high):
        lanes = pl.ds(2 * low, 2 * (high - low))
        for step in steps:
            peer = peers[step]
            copy = pltpu.make_async_remote_copy(
                src_ref=white.at[peer, :, :, lanes],
                dst_ref=own.at[me, :, :, lanes],
                send_sem=send_sem.at[c, step],
                recv_sem=recv_sem.at[c, step],
                device_id=(hour, chan, peer),
                device_id_type=MESH,
            )
            copy.start()
            sends[c, step] = copy

    loads[0].wait()
    for load in loads[2:]:
        load.start()
    for c, (low, high) in enumerate(chunks):
        size = high - low
        loads[1 + c].wait()
        values = samples[low:high].reshape(size * windows, samples.shape[2])
        product = jnp.dot(values, table[...], preferred_element_type=jnp.float32)
        for part in range(2):
            flat[part, : size * windows] = product[:, part * BINS : (part + 1) * BINS]
        for w in range(windows):
            pick = pl.ds(w, size, stride=windows)
            real = flat[0, pick, :].astype(jnp.bfloat16).T.astype(jnp.float32)
            imag = flat[1, pick, :].astype(jnp.bfloat16).T.astype(jnp.float32)
            packed = pack(*whiten(real, imag)).astype(jnp.bfloat16)
            white[:, w, :, 2 * low : 2 * high] = packed.reshape(count, local_bins, 2 * size)
        if c == 0:
            pl.semaphore_wait(barrier, count)
        send(c, far, low, high)
    forward(0, white.at[me], me)
    send(0, near, 0, samples_ref.shape[0])

    def settle(step):
        owner = peers[step]
        passes[step].wait_recv()
        source = own if step else white
        mine = source[owner].astype(jnp.float32).reshape(rows, white.shape[3])
        theirs = other[owner].astype(jnp.float32).reshape(rows, white.shape[3])
        for part in range(2):
            here, there = (
                jnp.concatenate([unpack(x[:, 2 * a : 2 * b], part) for a, b in chunks], axis=1)
                for x in (mine, theirs)
            )
            first_row = pl.multiple_of(part * total + owner * rows, 8)
            spread(mine_ref, first_row, here * scale)
            pair = [jnp.where(chan == 0, here, there), jnp.where(chan == 0, there, here)]
            spread(every_ref, first_row, jnp.concatenate(pair, axis=1))

    waiting = [0]
    for step in range(1, count):
        owner = peers[step]
        for c in range(n):
            if (c, step) in sends:
                sends[c, step].wait_recv()
        forward(step, own.at[owner], owner)
        waiting.append(step)
        if len(waiting) > 2:
            settle(waiting.pop(0))
    for step in waiting:
        settle(step)
    for copy in sends.values():
        copy.wait_send()
    for copy in passes.values():
        copy.wait_send()


def exchange(samples, table, count):
    channels, windows, length = samples.shape
    local_bins = BINS // count
    rows = 2 * windows * count * local_bins
    chunks = chunks_of(channels)
    n = len(chunks)
    blocks = pltpu.VMEM((count, windows, local_bins, 2 * channels), jnp.bfloat16)
    largest = max(high - low for low, high in chunks)
    pieces = pltpu.SemaphoreType.DMA((n, count))
    whole = pl.BlockSpec(memory_space=pltpu.VMEM)
    return pl.pallas_call(
        functools.partial(exchange_kernel, count),
        out_shape=(
            jax.ShapeDtypeStruct((pl.cdiv(channels, LANES), rows, LANES), jnp.float32),
            jax.ShapeDtypeStruct((pl.cdiv(2 * channels, LANES), rows, LANES), jnp.float32),
        ),
        in_specs=[pl.BlockSpec(memory_space=pltpu.HBM), pl.BlockSpec(memory_space=pltpu.HBM)],
        out_specs=(whole, whole),
        scratch_shapes=[
            pltpu.VMEM(samples.shape, samples.dtype),
            pltpu.VMEM(table.shape, table.dtype),
            pltpu.VMEM((2, largest * windows, BINS), jnp.float32),
            blocks,
            blocks,
            blocks,
            pltpu.SemaphoreType.DMA((n + 1,)),
            pieces,
            pieces,
            pltpu.SemaphoreType.DMA((count,)),
            pltpu.SemaphoreType.DMA((count,)),
        ],
        compiler_params=pltpu.CompilerParams(
            collective_id=0, has_side_effects=True, vmem_limit_bytes=40 << 20
        ),
        cost_estimate=pl.CostEstimate(
            flops=2 * samples.size * 2 * BINS, bytes_accessed=2 * samples.size, transcendentals=0
        ),
        name="exchange",
    )(samples, table)


def cross_kernel(mine_ref, every_ref, out_ref, held, sems):
    slots, step_bins, _, channels, width = held.shape
    step = pl.program_id(0)
    steps = out_ref.shape[1] // step_bins
    local_bins = steps * step_bins
    windows = mine_ref.shape[1] // (2 * local_bins)
    slot = lax.rem(step, slots)

    def copies(b, part, at_step, at_slot):
        return pltpu.make_async_copy(
            held.at[at_slot, b, part],
            out_ref.at[part, at_step * step_bins + b],
            sems.at[at_slot, b, part],
        )

    pieces = [(b, part) for b in range(step_bins) for part in range(2)]

    @pl.when(step >= slots)
    def _():
        for b, part in pieces:
            copies(b, part, step - slots, slot).wait()

    for b in range(step_bins):
        pick = pl.ds(step * step_bins + b, 2 * windows, stride=local_bins)
        here = [mine_ref[t, pick, :] for t in range(mine_ref.shape[0])]
        here = jnp.concatenate(here, axis=1)[:, :channels]
        left = here.astype(jnp.bfloat16)
        swapped = jnp.concatenate([here[windows:], -here[:windows]], axis=0).astype(jnp.bfloat16)
        right = [every_ref[t, pick, :].astype(jnp.bfloat16) for t in range(every_ref.shape[0])]
        right = jnp.concatenate(right, axis=1)[:, :width]
        for part, side in ((0, left), (1, swapped)):
            product = lax.dot_general(
                side, right, (((0,), (0,)), ((), ())), preferred_element_type=jnp.float32
            )
            held[slot, b, part] = product.astype(jnp.bfloat16)
            copies(b, part, step, slot).start()

    @pl.when(step == steps - 1)
    def _():
        for back in reversed(range(slots)):
            last = steps - 1 - back
            for b, part in pieces:
                copies(b, part, last, last % slots).wait()


def cross(mine, every, windows, channels):
    rows = mine.shape[1]
    local_bins = rows // (2 * windows)
    width = 2 * channels
    step_bins = 2 if local_bins % 2 == 0 else 1
    steps = local_bins // step_bins
    slots = min(2, steps)
    shape = (2, local_bins, channels, width)
    whole = pl.BlockSpec(memory_space=pltpu.VMEM)
    return pl.pallas_call(
        cross_kernel,
        grid=(steps,),
        out_shape=jax.ShapeDtypeStruct(shape, jnp.bfloat16),
        in_specs=[whole, whole],
        out_specs=pl.BlockSpec(memory_space=pl.ANY),
        scratch_shapes=[
            pltpu.VMEM((slots, step_bins, 2, channels, width), jnp.bfloat16),
            pltpu.SemaphoreType.DMA((slots, step_bins, 2)),
        ],
        compiler_params=pltpu.CompilerParams(vmem_limit_bytes=50 << 20),
        cost_estimate=pl.CostEstimate(
            flops=2 * rows * channels * width * 2,
            bytes_accessed=2 * math.prod(shape),
            transcendentals=0,
        ),
        name="cross",
    )(mine, every)


def local(samples):
    channels, windows, length = samples.shape
    count = lax.axis_size("freq")
    samples = pltpu.with_memory_space_constraint(samples, pltpu.HBM)
    table = pltpu.with_memory_space_constraint(bin_table(length, BINS), pltpu.HBM)
    mine, every = exchange(samples, table, count)
    return jnp.swapaxes(cross(mine, every, windows * count, channels), 2, 3)


def solution(mesh):
    return jax.shard_map(
        local,
        mesh=mesh,
        in_specs=(P("chan", ("hours", "freq"), None),),
        out_specs=P(None, ("hours", "freq"), None, "chan"),
        check_vma=False,
    )
```

```python
import functools
import math

import jax
import jax.numpy as jnp
import numpy as np
from jax import lax
from jax.experimental import pallas as pl
from jax.experimental.pallas import tpu as pltpu
from jax.sharding import PartitionSpec as P

BINS = 128
LANES = 128
MESH = pl.DeviceIdType.MESH


def bin_table(length, bins):
    position = np.arange(length, dtype=np.int64)[:, None]
    number = np.arange(bins, dtype=np.int64)[None, :] + 1
    step = np.float32(2.0 * math.pi / length)
    phase = (position * number % length).astype(np.float32) * step
    half = np.float32(0.5)
    taper = half - half * np.cos(position.astype(np.float32) * step)
    factor = np.float32(math.sqrt(8.0 / (3.0 * length)))
    table = np.concatenate([taper * np.cos(phase), -(taper * np.sin(phase))], axis=1) * factor
    return jnp.asarray(table.astype(np.float32)).astype(jnp.bfloat16)


def whiten(real, imag):
    bins = real.shape[0]
    power = real * real + imag * imag
    row = lax.broadcasted_iota(jnp.int32, (bins, 1), 0)
    summed = power
    for shift in (1, 2):
        summed = summed + jnp.where(row >= shift, pltpu.roll(power, shift, 0), 0.0)
        summed = summed + jnp.where(row < bins - shift, pltpu.roll(power, bins - shift, 0), 0.0)
    count = jnp.minimum(row + 2, bins - 1) - jnp.maximum(row - 2, 0) + 1
    level = jnp.maximum(summed * (1.0 / count.astype(jnp.float32)), 0.1)
    scale = lax.rsqrt(level)
    return real * scale, imag * scale


def chunks_of(channels):
    return ((0, LANES), (LANES, channels)) if channels > LANES else ((0, channels),)


def order_of(count):
    return sorted(range(1, count), key=lambda mask: (-mask.bit_length(), mask ^ (mask >> 1 & 1)))


def partner(me, mask, count):
    bits = count.bit_length() - 1
    other = 0
    for bit in range(bits):
        digit = lax.rem(me // (1 << bit), 2)
        other = other + (1 << bit) * ((1 - digit) if mask >> bit & 1 else digit)
    return other


def pack(real, imag):
    cut = real.shape[1] // LANES * LANES
    if cut == real.shape[1]:
        return jnp.concatenate([real, imag], axis=1)
    return jnp.concatenate([real[:, :cut], imag[:, :cut], real[:, cut:], imag[:, cut:]], axis=1)


def unpack(values, part):
    channels = values.shape[1] // 2
    cut = channels // LANES * LANES
    rest = channels - cut
    tail = 2 * cut + part * rest
    main = values[:, part * cut : (part + 1) * cut]
    return jnp.concatenate([main, values[:, tail : tail + rest]], axis=1) if rest else main


def spread(tiles, first_row, values):
    height, width = values.shape
    for t in range(pl.cdiv(width, LANES)):
        part = values[:, t * LANES : min((t + 1) * LANES, width)]
        if part.shape[1] < LANES:
            gap = jnp.zeros((height, LANES - part.shape[1]), part.dtype)
            part = jnp.concatenate([part, gap], axis=1)
        tiles[t, pl.ds(first_row, height), :] = part


def exchange_kernel(count, samples_ref, table_ref, mine_ref, every_ref, samples, table, flat,
                    white, own, other, load_sem, send_sem, recv_sem, pass_sem, got_sem):
    chunks = chunks_of(samples_ref.shape[0])
    n = len(chunks)
    hour = lax.axis_index("hours")
    chan = lax.axis_index("chan")
    me = lax.axis_index("freq")
    windows = samples_ref.shape[1]
    local_bins = BINS // count
    rows = windows * local_bins
    total = rows * count
    scale = 1.0 / (windows * count)
    steps = order_of(count)
    peers = {step: partner(me, step, count) for step in range(count)}

    loads = [pltpu.make_async_copy(table_ref, table, load_sem.at[n])]
    for c, (low, high) in enumerate(chunks):
        here = pl.ds(low, high - low)
        loads.append(pltpu.make_async_copy(samples_ref.at[here], samples.at[here], load_sem.at[c]))
    for load in loads[:2]:
        load.start()

    barrier = pltpu.get_barrier_semaphore()
    for step in steps:
        peer = peers[step]
        pl.semaphore_signal(barrier, inc=1, device_id=(hour, chan, peer), device_id_type=MESH)
    pl.semaphore_signal(barrier, inc=1, device_id=(hour, 1 - chan, me), device_id_type=MESH)

    sends, passes = {}, {}

    def forward(step, source_ref, owner):
        copy = pltpu.make_async_remote_copy(
            src_ref=source_ref,
            dst_ref=other.at[owner],
            send_sem=pass_sem.at[step],
            recv_sem=got_sem.at[step],
            device_id=(hour, 1 - chan, me),
            device_id_type=MESH,
        )
        copy.start()
        passes[step] = copy

    far = [step for step in steps if 2 * step >= count]
    near = [step for step in steps if 2 * step < count]

    def send(c, steps, low, high):
        lanes = pl.ds(2 * low, 2 * (high - low))
        for step in steps:
            peer = peers[step]
            copy = pltpu.make_async_remote_copy(
                src_ref=white.at[peer, :, :, lanes],
                dst_ref=own.at[me, :, :, lanes],
                send_sem=send_sem.at[c, step],
                recv_sem=recv_sem.at[c, step],
                device_id=(hour, chan, peer),
                device_id_type=MESH,
            )
            copy.start()
            sends[c, step] = copy

    loads[0].wait()
    for load in loads[2:]:
        load.start()
    for c, (low, high) in enumerate(chunks):
        size = high - low
        loads[1 + c].wait()
        values = samples[low:high].reshape(size * windows, samples.shape[2])
        product = jnp.dot(values, table[...], preferred_element_type=jnp.float32)
        for part in range(2):
            flat[part, : size * windows] = product[:, part * BINS : (part + 1) * BINS]
        for w in range(windows):
            pick = pl.ds(w, size, stride=windows)
            real = flat[0, pick, :].astype(jnp.bfloat16).T.astype(jnp.float32)
            imag = flat[1, pick, :].astype(jnp.bfloat16).T.astype(jnp.float32)
            packed = pack(*whiten(real, imag)).astype(jnp.bfloat16)
            white[:, w, :, 2 * low : 2 * high] = packed.reshape(count, local_bins, 2 * size)
        if c == 0:
            pl.semaphore_wait(barrier, count)
        if c == n - 1:
            send(0, near, 0, high)
        send(c, far, low, high)
    forward(0, white.at[me], me)

    def settle(step):
        owner = peers[step]
        passes[step].wait_recv()
        source = own if step else white
        mine = source[owner].astype(jnp.float32).reshape(rows, white.shape[3])
        theirs = other[owner].astype(jnp.float32).reshape(rows, white.shape[3])
        for part in range(2):
            here, there = (
                jnp.concatenate([unpack(x[:, 2 * a : 2 * b], part) for a, b in chunks], axis=1)
                for x in (mine, theirs)
            )
            first_row = pl.multiple_of(part * total + owner * rows, 8)
            spread(mine_ref, first_row, here * scale)
            pair = [jnp.where(chan == 0, here, there), jnp.where(chan == 0, there, here)]
            spread(every_ref, first_row, jnp.concatenate(pair, axis=1))

    waiting = [0]
    for step in range(1, count):
        owner = peers[step]
        for c in range(n):
            if (c, step) in sends:
                sends[c, step].wait_recv()
        forward(step, own.at[owner], owner)
        waiting.append(step)
        if len(waiting) > 2:
            settle(waiting.pop(0))
    for step in waiting:
        settle(step)
    for copy in sends.values():
        copy.wait_send()
    for copy in passes.values():
        copy.wait_send()


def exchange(samples, table, count):
    channels, windows, length = samples.shape
    local_bins = BINS // count
    rows = 2 * windows * count * local_bins
    chunks = chunks_of(channels)
    n = len(chunks)
    blocks = pltpu.VMEM((count, windows, local_bins, 2 * channels), jnp.bfloat16)
    largest = max(high - low for low, high in chunks)
    pieces = pltpu.SemaphoreType.DMA((n, count))
    whole = pl.BlockSpec(memory_space=pltpu.VMEM)
    return pl.pallas_call(
        functools.partial(exchange_kernel, count),
        out_shape=(
            jax.ShapeDtypeStruct((pl.cdiv(channels, LANES), rows, LANES), jnp.float32),
            jax.ShapeDtypeStruct((pl.cdiv(2 * channels, LANES), rows, LANES), jnp.float32),
        ),
        in_specs=[pl.BlockSpec(memory_space=pltpu.HBM), pl.BlockSpec(memory_space=pltpu.HBM)],
        out_specs=(whole, whole),
        scratch_shapes=[
            pltpu.VMEM(samples.shape, samples.dtype),
            pltpu.VMEM(table.shape, table.dtype),
            pltpu.VMEM((2, largest * windows, BINS), jnp.float32),
            blocks,
            blocks,
            blocks,
            pltpu.SemaphoreType.DMA((n + 1,)),
            pieces,
            pieces,
            pltpu.SemaphoreType.DMA((count,)),
            pltpu.SemaphoreType.DMA((count,)),
        ],
        compiler_params=pltpu.CompilerParams(
            collective_id=0, has_side_effects=True, vmem_limit_bytes=40 << 20
        ),
        cost_estimate=pl.CostEstimate(
            flops=2 * samples.size * 2 * BINS, bytes_accessed=2 * samples.size, transcendentals=0
        ),
        name="exchange",
    )(samples, table)


def cross_kernel(mine_ref, every_ref, out_ref, held, sems):
    slots, step_bins, _, channels, width = held.shape
    step = pl.program_id(0)
    steps = out_ref.shape[1] // step_bins
    local_bins = steps * step_bins
    windows = mine_ref.shape[1] // (2 * local_bins)
    slot = lax.rem(step, slots)

    def copies(b, part, at_step, at_slot):
        return pltpu.make_async_copy(
            held.at[at_slot, b, part],
            out_ref.at[part, at_step * step_bins + b],
            sems.at[at_slot, b, part],
        )

    pieces = [(b, part) for b in range(step_bins) for part in range(2)]

    @pl.when(step >= slots)
    def _():
        for b, part in pieces:
            copies(b, part, step - slots, slot).wait()

    for b in range(step_bins):
        pick = pl.ds(step * step_bins + b, 2 * windows, stride=local_bins)
        here = [mine_ref[t, pick, :] for t in range(mine_ref.shape[0])]
        here = jnp.concatenate(here, axis=1)[:, :channels]
        left = here.astype(jnp.bfloat16)
        swapped = jnp.concatenate([here[windows:], -here[:windows]], axis=0).astype(jnp.bfloat16)
        right = [every_ref[t, pick, :].astype(jnp.bfloat16) for t in range(every_ref.shape[0])]
        right = jnp.concatenate(right, axis=1)[:, :width]
        for part, side in ((0, left), (1, swapped)):
            product = lax.dot_general(
                side, right, (((0,), (0,)), ((), ())), preferred_element_type=jnp.float32
            )
            held[slot, b, part] = product.astype(jnp.bfloat16)
            copies(b, part, step, slot).start()

    @pl.when(step == steps - 1)
    def _():
        for back in reversed(range(slots)):
            last = steps - 1 - back
            for b, part in pieces:
                copies(b, part, last, last % slots).wait()


def cross(mine, every, windows, channels):
    rows = mine.shape[1]
    local_bins = rows // (2 * windows)
    width = 2 * channels
    step_bins = 2 if local_bins % 2 == 0 else 1
    steps = local_bins // step_bins
    slots = min(2, steps)
    shape = (2, local_bins, channels, width)
    whole = pl.BlockSpec(memory_space=pltpu.VMEM)
    return pl.pallas_call(
        cross_kernel,
        grid=(steps,),
        out_shape=jax.ShapeDtypeStruct(shape, jnp.bfloat16),
        in_specs=[whole, whole],
        out_specs=pl.BlockSpec(memory_space=pl.ANY),
        scratch_shapes=[
            pltpu.VMEM((slots, step_bins, 2, channels, width), jnp.bfloat16),
            pltpu.SemaphoreType.DMA((slots, step_bins, 2)),
        ],
        compiler_params=pltpu.CompilerParams(vmem_limit_bytes=50 << 20),
        cost_estimate=pl.CostEstimate(
            flops=2 * rows * channels * width * 2,
            bytes_accessed=2 * math.prod(shape),
            transcendentals=0,
        ),
        name="cross",
    )(mine, every)


def local(samples):
    channels, windows, length = samples.shape
    count = lax.axis_size("freq")
    samples = pltpu.with_memory_space_constraint(samples, pltpu.HBM)
    table = pltpu.with_memory_space_constraint(bin_table(length, BINS), pltpu.HBM)
    mine, every = exchange(samples, table, count)
    return jnp.swapaxes(cross(mine, every, windows * count, channels), 2, 3)


def solution(mesh):
    return jax.shard_map(
        local,
        mesh=mesh,
        in_specs=(P("chan", ("hours", "freq"), None),),
        out_specs=P(None, ("hours", "freq"), None, "chan"),
        check_vma=False,
    )
```
